512 devices in a mesh: shard: 128 (over y, z, core), blk: 4 (over x).
Axes of the slice: x: 4, y: 8, z: 8, core: 2. Of those that a mesh axis runs over, the one named last changes fastest.
Arguments:
- queries: bfloat16 [256, 32, 128], P('shard'), may hold values from -0.5 to 0.5
- passages: bfloat16 [8192, 128, 128], P('shard', 'blk'), may hold values from -0.5 to 0.5
- lengths: int32 [8192], P('shard'), may hold values from 16 to 128, as said below
- pair_query: int32 [16384, 12], P('shard'), may hold values from 0 to 1
- pair_passage: int32 [16384, 12], P('shard'), may hold values from 0 to 63
- send_counts: int32 [16384], P('shard'), may hold values from 1 to 12, as said below
Outputs:
- pair_scores: float32 [16384, 12], P('shard')
The draws below stay inside these ranges and needn't reach their ends.
Inputs may be any that keep to these rules, and one draw needn't show every extreme that they name: `lengths`: every passage has at least 16 tokens; some passage has exactly 128. `send_counts`: every route has at least one live slot; in every draw one passage owner receives 12 live pairs from every query owner.
All inputs are finite; a program needn't handle non-finite values.
Results may differ from the reference program's by a relative error of at most 0.0003.
Values may be sent and summed in bfloat16 or wider, within the bound.
A program may use at most 64 MiB of HBM per device.

```python
import math
import jax
import jax.numpy as jnp
from jax import lax

DIM = 128
QLEN = 32
PLEN = 128
Q_DEV = 2
PASSAGES_PER_HOST = 64
SLOT = 12
QUERIES = 256
PASSAGES = 8192
OWNER_PAIRS = 16384
N_SHARD = 128


def draw_lengths(key, part):
    key = jax.random.fold_in(key, 13)
    first, second = jax.random.split(key)
    values = jax.random.randint(first, (PASSAGES,), PLEN // 8, PLEN + 1)
    chosen = jax.random.randint(second, (), 0, PASSAGES)
    return values.at[chosen].set(PLEN).astype(jnp.int32)


def draw_send_counts(key, part):
    key = jax.random.fold_in(key, 11)
    first, second = jax.random.split(key)
    counts = jax.random.randint(first, (N_SHARD, N_SHARD), 1, SLOT)
    hottest = jax.random.randint(second, (), 0, N_SHARD)
    column = jnp.arange(N_SHARD, dtype=jnp.int32)[None, :]
    counts = jnp.where(column == hottest, SLOT, counts)
    return counts.reshape(OWNER_PAIRS).astype(jnp.int32)


def place_ends(values, stream_key, low, high):
    spot = [jax.random.randint(jax.random.fold_in(stream_key, axis), (), 0, length) for axis, length in enumerate(values.shape)]
    main_axis = values.shape.index(max(values.shape))
    next_to = spot[:main_axis] + [(spot[main_axis] + 1) % values.shape[main_axis]] + spot[main_axis + 1:]
    return values.at[tuple(spot)].set(low).at[tuple(next_to)].set(high)


def shard_levels(rng, shape, cuts, low, high):
    def one(axis_at, parts):
        heights = jax.random.uniform(jax.random.fold_in(jax.random.fold_in(rng, 6), axis_at), (parts,), jnp.float32, low / len(cuts), high / len(cuts))
        return jnp.repeat(jnp.exp(heights), shape[axis_at] // parts).reshape((-1,) + (1,) * (len(shape) - axis_at - 1))

    gain = one(*cuts[0])
    for cut in cuts[1:]:
        gain = gain * one(*cut)
    return gain


def gaussian(stream_key, dims, deviation, most, cuts=(), kind=jnp.bfloat16):
    result = jax.random.normal(stream_key, dims, jnp.float32) * deviation
    if len(cuts) > 0:
        result = shard_levels(stream_key, dims, cuts, -0.22, 0.18) * result
    return jnp.clip(result, min=-most, max=most).astype(kind)


def setup_inputs(seed: int = 0) -> dict:
    key_list = jax.random.split(jax.random.key(seed), 7)
    queries = gaussian(key_list[0], (QUERIES, QLEN, DIM), 0.09, 0.5, ((0, 128),))
    passages = gaussian(key_list[1], (PASSAGES, PLEN, DIM), 0.09, 0.5, ((0, 128), (1, 4)))
    lengths = draw_lengths(jax.random.fold_in(key_list[6], 71), 0)
    pair_query = place_ends(jax.random.randint(key_list[3], (OWNER_PAIRS, SLOT), 0, Q_DEV), jax.random.fold_in(key_list[3], 1), 0, Q_DEV - 1).astype(jnp.int32)
    pair_passage = place_ends(jax.random.randint(key_list[4], (OWNER_PAIRS, SLOT), 0, PASSAGES_PER_HOST), jax.random.fold_in(key_list[4], 1), 0, PASSAGES_PER_HOST - 1).astype(jnp.int32)
    send_counts = draw_send_counts(jax.random.fold_in(key_list[6], 71), 0)
    return {"queries": queries, "passages": passages, "lengths": lengths, "pair_query": pair_query, "pair_passage": pair_passage, "send_counts": send_counts}


def reference(queries, passages, lengths, pair_query, pair_passage, send_counts):
    route = jnp.arange(OWNER_PAIRS, dtype=jnp.int32)
    sender_owner = route // N_SHARD
    target = route % N_SHARD
    query_ids = (pair_query + (sender_owner * Q_DEV)[:, None]).reshape(-1)
    passage_ids = (pair_passage + (target * PASSAGES_PER_HOST)[:, None]).reshape(-1)
    total = OWNER_PAIRS * SLOT
    width = math.gcd(total, 256)

    def score_block(ids):
        qid, pid = ids
        query_tile_rows = queries[qid].astype(jnp.float32)
        token_tile_rows = passages[pid].astype(jnp.float32)
        match_scores = jnp.einsum("oer,ogr->oeg", query_tile_rows, token_tile_rows)
        live = jnp.arange(PLEN, dtype=jnp.int32)[None, :] < lengths[pid][:, None]
        match_scores = jnp.where(live[:, None, :], match_scores, -1e30)
        return jnp.sum(jnp.max(match_scores, axis=2), axis=1)

    totals = lax.map(score_block, (query_ids.reshape(-1, width), passage_ids.reshape(-1, width)))
    totals = totals.reshape(OWNER_PAIRS, SLOT)
    valid = jnp.arange(SLOT, dtype=jnp.int32)[None, :] < send_counts[:, None]
    return jnp.where(valid, totals, 0.0).astype(jnp.float32)
```

```python
import functools
import math

import jax
import jax.numpy as jnp
from jax import lax
from jax.experimental import pallas as pl
from jax.experimental.pallas import tpu as pltpu
from jax.sharding import PartitionSpec as P

NT = (((1,), (1,)), ((), ()))

def kernel(side, xs, q_dev, q_ref, p_ref, len_ref, pq_ref, pp_ref, cnt_ref, o_ref,
           qs, ps, w, wx, rows, table, idx, outs,
           qa_send, qa_recv, ring_send, ring_recv, sib_send, sib_recv,
           px_send, px_recv, px_local, wx_send, wx_recv, row_send, row_recv, out_send, out_recv):
    me = lax.axis_index("shard")
    x = lax.axis_index("blk")
    core = me % 2
    zz = (me // 2) % side
    yy = me // (2 * side)
    f = zz + core * (yy - zz)
    g = yy + core * (zz - yy)

    def owner(c, ff, gg):
        return c + ff * (2 + c * (2 * side - 2)) + gg * (2 * side - c * (2 * side - 2))

    def wrap(value, size):
        return (value + 2 * size) % size

    sibling = {"shard": me + 1 - 2 * core}

    def first(o):
        return {"shard": owner(core, wrap(f + o, side), g)}

    def second(o):
        return {"shard": owner(core, f, wrap(g + o, side))}

    def along_x(o):
        return {"blk": wrap(x + o, xs)}

    barrier = pltpu.get_barrier_semaphore()
    near = sorted({1 % side, (side - 1) % side})
    friends = ([first(o) for o in range(1, side)] + [second(o) for o in near] + [sibling]
               + [along_x(o) for o in range(1, xs)])
    for friend in friends:
        pl.semaphore_signal(barrier, inc=1, device_id=friend, device_id_type=pl.DeviceIdType.MESH)
    pl.semaphore_wait(barrier, len(friends))

    def remote(src, dst, send, recv, to):
        return pltpu.make_async_remote_copy(src_ref=src, dst_ref=dst, send_sem=send, recv_sem=recv,
                                            device_id=to, device_id_type=pl.DeviceIdType.MESH)

    held = ps.shape[0]
    q_rows = q_ref.shape[0]

    qa = [remote(q_ref, qs.at[core, g, f], qa_send.at[o], qa_recv.at[o], first(o)) for o in range(1, side)]
    for copy in qa:
        copy.start()
    px = [remote(p_ref.at[pl.ds(wrap(x + o, xs) * held, held)], ps.at[:, x], px_send.at[o], px_recv.at[o],
                 along_x(o)) for o in range(1, xs)]
    for copy in px:
        copy.start()
    px_own = pltpu.make_async_copy(p_ref.at[pl.ds(x * held, held)], ps.at[:, x], px_local)
    px_own.start()
    qs[core, g, f] = q_ref[...]

    slots = pq_ref.shape[0]
    wanted = pq_ref[...] * (held * xs) + pp_ref[...]
    owners = wanted.shape[1]
    wanted = jnp.concatenate([wanted, jnp.zeros((128 - slots, owners), jnp.int32)], axis=0)
    idx[...] = wanted.T

    n = side * q_rows

    tokens = q_rows // q_dev
    lane = lax.broadcasted_iota(jnp.int32, (q_dev * side, n), 1)
    line = lax.broadcasted_iota(jnp.int32, (q_dev * side, n), 0)
    member = jnp.where((line % side) * q_dev + line // side == lane // tokens, 1.0, 0.0).astype(jnp.bfloat16)

    plen = ps.shape[1] * ps.shape[2]
    dim = ps.shape[3]

    def score(c, gg):
        queries = qs[c, gg].reshape(n, dim)
        sims = lax.dot_general(ps[...].reshape(held * plen, dim), queries, NT, preferred_element_type=jnp.float32)
        best = jnp.max(sims.reshape(held, plen, n), axis=1)
        high = best.astype(jnp.bfloat16)
        rest = best - high.astype(jnp.float32)
        mid = rest.astype(jnp.bfloat16)
        low = (rest - mid.astype(jnp.float32)).astype(jnp.bfloat16)
        total = (lax.dot_general(member, high, NT, preferred_element_type=jnp.float32)
                 + lax.dot_general(member, mid, NT, preferred_element_type=jnp.float32)
                 + lax.dot_general(member, low, NT, preferred_element_type=jnp.float32))
        blank = jnp.zeros((side, 128 - held), jnp.float32)
        line_w = jnp.zeros((side, 128), jnp.float32)
        for q in range(q_dev):
            part = jnp.concatenate([total[q * side:(q + 1) * side], blank], axis=1)
            line_w = line_w + pltpu.roll(part, q * held * xs + x * held, 1)
        w[c, gg] = line_w

    def place(m):
        return wrap(g - (2 * (m % 2) - 1) * ((m + 1) // 2), side)

    def sib_place(m):
        return wrap(f - (2 * (m % 2) - 1) * ((m + 1) // 2), side)

    def pass_on(m, at, way):
        slab = qs.at[core, at]
        return remote(slab, slab, ring_send, ring_recv.at[m + 2], second(way))

    def to_sibling(m, at):
        slab = qs.at[core, at]
        return remote(slab, slab, sib_send, sib_recv.at[m], sibling)

    for copy in qa:
        copy.wait_recv()
    remote(qs.at[core, g], qs.at[core, g], ring_send, ring_recv.at[1], second(1)).start()
    if side > 2:
        remote(qs.at[core, g], qs.at[core, g], ring_send, ring_recv.at[2], second(-1)).start()
    to_sibling(0, g).start()

    px_own.wait()
    for copy in px:
        copy.wait_recv()
    def pad(i, _):
        token = lax.broadcasted_iota(jnp.int32, (plen, dim), 0)
        vectors = ps[i].reshape(plen, dim).astype(jnp.float32)
        kept = jnp.where(token < len_ref[x * held + i], vectors, vectors[0:1, :])
        ps[i] = kept.astype(jnp.bfloat16).reshape(ps.shape[1:])
        return 0
    lax.fori_loop(0, held, pad, 0)

    score(core, g)

    def step(m, _):
        at = place(m)
        slab = qs.at[core, at]
        remote(slab, slab, ring_send, ring_recv.at[m], sibling).wait_recv()

        @pl.when(m <= side - 3)
        def _():
            pass_on(m, at, 2 * (m % 2) - 1).start()

        to_sibling(m, at).start()
        other = sib_place(m - 1)
        slab = qs.at[1 - core, other]
        remote(slab, slab, sib_send, sib_recv.at[m - 1], sibling).wait_recv()
        score(core, at)
        score(1 - core, other)
        return 0
    lax.fori_loop(1, side, step, 0)
    last = sib_place(side - 1)
    slab = qs.at[1 - core, last]
    remote(slab, slab, sib_send, sib_recv.at[side - 1], sibling).wait_recv()
    score(1 - core, last)

    share = side // xs
    wxs = [remote(w.at[:, pl.ds(wrap(x + o, xs) * share, share)], wx.at[o], wx_send.at[o], wx_recv.at[o], along_x(o))
           for o in range(1, xs)]
    for copy in wxs:
        copy.start()
    full = w[:, pl.ds(x * share, share)]
    for o, copy in zip(range(1, xs), wxs):
        copy.wait_recv()
        full = full + wx[o]
    targets = 2 * share * side
    rows[...] = full.reshape(targets, 1, 128)

    def row(k, _):
        k = (k + me) % targets
        to = owner(k // (share * side), k % side, x * share + (k // side) % share)

        @pl.when(to != me)
        def _():
            remote(rows.at[k], table.at[me], row_send, row_recv, {"shard": to}).start()

        @pl.when(to == me)
        def _():
            table[me] = rows[k]
        return 0
    lax.fori_loop(0, targets, row, 0)

    home = g // share
    out_copies = [remote(outs, outs, out_send.at[o], out_recv, along_x(o)) for o in range(1, xs)]

    @pl.when(home == x)
    def _():
        lead = table.at[pl.ds(0, owners - 1)]
        remote(lead, lead, row_send, row_recv, sibling).wait_recv()
        picked = jnp.take_along_axis(table[...].reshape(owners, 128), idx[...], axis=1, mode="promise_in_bounds")
        picked = picked.T[:slots, :]
        slot = lax.broadcasted_iota(jnp.int32, (slots, owners), 0)
        outs[...] = jnp.where(slot < cnt_ref[...], picked, 0.0)
        for copy in out_copies:
            copy.start()
        o_ref[...] = outs[...]
        for copy in out_copies:
            copy.wait_send()
        lead = rows.at[pl.ds(0, targets - 1)]
        remote(lead, lead, row_send, row_recv, sibling).wait_send()

    @pl.when(home != x)
    def _():
        out_copies[0].wait_recv()
        o_ref[...] = outs[...]
        remote(rows, rows, row_send, row_recv, sibling).wait_send()

    for copy in qa:
        copy.wait_send()
    for copy in px:
        copy.wait_send()
    for copy in wxs:
        copy.wait_send()
    lead = qs.at[core, pl.ds(0, side - 1)]
    remote(lead, lead, ring_send, ring_recv.at[0], sibling).wait_send()
    remote(qs.at[core], qs.at[core], sib_send, sib_recv.at[0], sibling).wait_send()

def local(side, xs, queries, passages, lengths, pair_query, pair_passage, send_counts):
    owners, slots = pair_query.shape
    q_dev, q_tokens, dim = queries.shape
    per_owner, block, _ = passages.shape
    held = per_owner // xs
    share = side // xs
    vmem = pl.BlockSpec(memory_space=pltpu.VMEM)
    dma = pltpu.SemaphoreType.DMA
    out = pl.pallas_call(
        functools.partial(kernel, side, xs, q_dev),
        out_shape=jax.ShapeDtypeStruct((slots, owners), jnp.float32),
        in_specs=[vmem, pl.BlockSpec(memory_space=pl.ANY), pl.BlockSpec(memory_space=pltpu.SMEM), vmem, vmem, vmem],
        out_specs=vmem,
        scratch_shapes=[
            pltpu.VMEM((2, side, side, q_dev * q_tokens, dim), jnp.bfloat16),
            pltpu.VMEM((held, xs, block, dim), jnp.bfloat16),
            pltpu.VMEM((2, side, side, 128), jnp.float32),
            pltpu.VMEM((xs, 2, share, side, 128), jnp.float32),
            pltpu.VMEM((2 * share * side, 1, 128), jnp.float32),
            pltpu.VMEM((owners, 1, 128), jnp.float32),
            pltpu.VMEM((owners, 128), jnp.int32),
            pltpu.VMEM((slots, owners), jnp.float32),
            dma((side,)), dma((side,)), dma, dma((side + 2,)), dma, dma((side,)),
            dma((xs,)), dma((xs,)), dma, dma((xs,)), dma((xs,)), dma, dma, dma((xs,)), dma,
        ],
        compiler_params=pltpu.CompilerParams(
            collective_id=0, has_side_effects=True, vmem_limit_bytes=48 * 2**20),
        cost_estimate=pl.CostEstimate(
            flops=2 * per_owner * block * owners * q_dev * q_tokens * dim, bytes_accessed=8 * 2**20,
            transcendentals=0),
    )(queries.reshape(q_dev * q_tokens, dim), passages, lengths,
      pair_query.T, pair_passage.T, send_counts.reshape(1, owners))
    return out.T

def solution(mesh):
    placed = (
        P("shard", None, None),
        P("shard", "blk", None),
        P("shard"),
        P("shard", None),
        P("shard", None),
        P("shard"),
    )
    side = math.isqrt(mesh.shape["shard"] // 2)
    return jax.shard_map(
        functools.partial(local, side, mesh.shape["blk"]),
        mesh=mesh, in_specs=placed, out_specs=P("shard", None), check_vma=False
    )
```

```python
import functools
import math

import jax
import jax.numpy as jnp
from jax import lax
from jax.experimental import pallas as pl
from jax.experimental.pallas import tpu as pltpu
from jax.sharding import PartitionSpec as P

NT = (((1,), (1,)), ((), ()))
ORDER = (0, 4, 1, 2, -2, 3, -3, -1)


def kernel(side, xs, q_dev, q_hbm, p_hbm, len_hbm, pq_hbm, pp_hbm, cnt_hbm, o_ref,
           len_ref, pq_ref, pp_ref, cnt_ref, qs, ps, rows, table, idx, outs,
           in_sems, near_send, near_recv, far_recv, opp_send, opp_recv, ring_send, ring_recv, sib_send, sib_recv,
           px_send, px_recv, px_local, row_send, row_recv, out_send, out_recv):
    me = lax.axis_index("shard")
    x = lax.axis_index("blk")
    core = me % 2
    zz = (me // 2) % side
    yy = me // (2 * side)
    f = zz + core * (yy - zz)
    g = yy + core * (zz - yy)
    half = side // 2

    def wrap(value, size):
        return (value + 2 * size) % size

    def at(ff, gg):
        ff, gg = wrap(ff, side), wrap(gg, side)
        return {"shard": core + ff * (2 + core * (2 * side - 2)) + gg * (2 * side - core * (2 * side - 2))}

    def along_x(o):
        return {"blk": wrap(x + o, xs)}

    sibling = {"shard": me + 1 - 2 * core}

    def remote(src, dst, send, recv, to):
        return pltpu.make_async_remote_copy(src_ref=src, dst_ref=dst, send_sem=send, recv_sem=recv,
                                            device_id=to, device_id_type=pl.DeviceIdType.MESH)

    sources = [(len_hbm, len_ref), (pq_hbm, pq_ref), (pp_hbm, pp_ref), (cnt_hbm, cnt_ref), (q_hbm, qs.at[g, f])]
    small = [pltpu.make_async_copy(src, dst, in_sems.at[i]) for i, (src, dst) in enumerate(sources)]
    for copy in small:
        copy.start()

    barrier = pltpu.get_barrier_semaphore()
    friends = ([at(f + o, g) for o in range(1, side)] + [at(f, g + o) for o in (1, -1, 2, -2, half)] + [sibling]
               + [along_x(o) for o in range(1, xs)])
    for friend in friends:
        pl.semaphore_signal(barrier, inc=1, device_id=friend, device_id_type=pl.DeviceIdType.MESH)
    pl.semaphore_wait(barrier, len(friends))

    held = ps.shape[1]
    q_rows = q_hbm.shape[0]

    remote(q_hbm, qs.at[g, f], near_send, far_recv, at(f, g + half)).start()
    for o in range(1, side):
        remote(q_hbm, qs.at[g, f], near_send, near_recv, at(f + o, g)).start()
    px = [remote(p_hbm.at[pl.ds(wrap(x + o, xs) * held, held)], ps.at[core, :, x], px_send.at[o], px_recv.at[o],
                 along_x(o)) for o in range(1, xs)]
    for copy in px:
        copy.start()
    px_own = pltpu.make_async_copy(p_hbm.at[pl.ds(x * held, held)], ps.at[core, :, x], px_local)
    px_own.start()

    for copy in small:
        copy.wait()
    slots = pq_ref.shape[0]
    wanted = pq_ref[...] * (held * xs) + pp_ref[...]
    owners = wanted.shape[1]
    wanted = jnp.concatenate([wanted, jnp.zeros((128 - slots, owners), jnp.int32)], axis=0)
    idx[...] = wanted.T

    n = side * q_rows
    tokens = q_rows // q_dev
    lane = lax.broadcasted_iota(jnp.int32, (q_dev * side, n), 1)
    line = lax.broadcasted_iota(jnp.int32, (q_dev * side, n), 0)
    member = jnp.where((line % side) * q_dev + line // side == lane // tokens, 1.0, 0.0).astype(jnp.bfloat16)

    plen = ps.shape[2] * ps.shape[3]
    dim = ps.shape[4]

    def score(gg, c):
        queries = qs[gg].reshape(n, dim)
        sims = lax.dot_general(ps[c].reshape(held * plen, dim), queries, NT, preferred_element_type=jnp.float32)
        best = jnp.max(sims.reshape(held, plen, n), axis=1)
        high = best.astype(jnp.bfloat16)
        rest = best - high.astype(jnp.float32)
        mid = rest.astype(jnp.bfloat16)
        low = (rest - mid.astype(jnp.float32)).astype(jnp.bfloat16)
        total = (lax.dot_general(member, high, NT, preferred_element_type=jnp.float32)
                 + lax.dot_general(member, mid, NT, preferred_element_type=jnp.float32)
                 + lax.dot_general(member, low, NT, preferred_element_type=jnp.float32))
        blank = jnp.zeros((side, 128 - held), jnp.float32)
        line_w = jnp.zeros((side, 128), jnp.float32)
        for q in range(q_dev):
            part = jnp.concatenate([total[q * side:(q + 1) * side], blank], axis=1)
            line_w = line_w + pltpu.roll(part, q * held * xs + x * held, 1)
        rows[c, gg] = line_w.reshape(side, 1, 128)

    def send_rows(gg, start):
        for o in range(start, side):
            ff = wrap(f + o, side)
            remote(rows.at[:, gg, ff], table.at[pl.ds(2 * (me // 2), 2)], row_send, row_recv, at(ff, gg)).start()

    def arrived(gg, d):
        remote(qs.at[gg], qs.at[gg], ring_send, ring_recv.at[d], sibling).wait_recv()

    def pass_on(gg, o):
        remote(qs.at[gg], qs.at[gg], ring_send, ring_recv.at[wrap(gg - g - o, side)], at(f, g + o)).start()

    opposite = wrap(g + half, side)
    remote(q_hbm, qs.at[opposite, f], near_send, far_recv, sibling).wait_recv()
    for o in range(1, side):
        remote(qs.at[opposite, f], qs.at[opposite, f], opp_send, opp_recv, at(f + o, g)).start()
    seven = qs.at[g, pl.ds(0, side - 1)]
    remote(seven, seven, near_send, near_recv, sibling).wait_recv()
    for o in (1, -1, 2, -2):
        pass_on(g, o)

    px_own.wait()
    for copy in px:
        copy.wait_recv()

    def pad(i, _):
        token = lax.broadcasted_iota(jnp.int32, (plen, dim), 0)
        vectors = ps[core, i].reshape(plen, dim).astype(jnp.float32)
        kept = jnp.where(token < len_ref[x * held + i], vectors, vectors[0:1, :])
        ps[core, i] = kept.astype(jnp.bfloat16).reshape(ps.shape[2:])
        return 0
    lax.fori_loop(0, held, pad, 0)
    share = remote(ps.at[core], ps.at[core], sib_send, sib_recv, sibling)
    share.start()

    score(g, core)
    remote(seven, seven, opp_send, opp_recv, sibling).wait_recv()
    for o in (1, -1):
        pass_on(opposite, o)
    share.wait_recv()
    score(g, 1 - core)
    send_rows(g, 1)
    table[pl.ds(2 * (me // 2), 2)] = rows[:, g, f]

    def step(k, _):
        d = sum(jnp.where(k == i, o, 0) for i, o in enumerate(ORDER))
        gg = wrap(g + d, side)

        @pl.when(k > 1)
        def _():
            arrived(gg, wrap(d, side))
        score(gg, core)
        score(gg, 1 - core)
        send_rows(gg, 0)
        return 0
    lax.fori_loop(1, side, step, 0)

    rest = table.at[pl.ds(0, owners - 2)]
    remote(rest, rest, row_send, row_recv, sibling).wait_recv()
    picked = jnp.take_along_axis(table[...].reshape(owners, 128), idx[...], axis=1, mode="promise_in_bounds")
    picked = picked.T[:slots, :]
    slot = lax.broadcasted_iota(jnp.int32, (slots, owners), 0)
    outs[0] = jnp.where(slot < cnt_ref[...], picked, 0.0)
    out_copies = [remote(outs.at[0], outs.at[o], out_send.at[o], out_recv.at[o], along_x(o)) for o in range(1, xs)]
    for copy in out_copies:
        copy.start()
    total = outs[0]
    for o, copy in zip(range(1, xs), out_copies):
        copy.wait_recv()
        total = total + outs[o]
    o_ref[...] = total

    for copy in out_copies + px + [share]:
        copy.wait_send()
    remote(qs.at[g], qs.at[g], near_send, far_recv, sibling).wait_send()
    remote(seven, seven, opp_send, opp_recv, sibling).wait_send()
    six = qs.at[pl.ds(0, 6)]
    remote(six, six, ring_send, ring_recv.at[0], sibling).wait_send()
    remote(rest, rest, row_send, row_recv, sibling).wait_send()


def local(side, xs, queries, passages, lengths, pair_query, pair_passage, send_counts):
    owners, slots = pair_query.shape
    q_dev, q_tokens, dim = queries.shape
    per_owner, block, _ = passages.shape
    held = per_owner // xs
    dma = pltpu.SemaphoreType.DMA
    out = pl.pallas_call(
        functools.partial(kernel, side, xs, q_dev),
        out_shape=jax.ShapeDtypeStruct((slots, owners), jnp.float32),
        in_specs=[pl.BlockSpec(memory_space=pltpu.HBM)] * 6,
        out_specs=pl.BlockSpec(memory_space=pltpu.VMEM),
        scratch_shapes=[
            pltpu.SMEM((per_owner,), jnp.int32),
            pltpu.VMEM((slots, owners), jnp.int32),
            pltpu.VMEM((slots, owners), jnp.int32),
            pltpu.VMEM((1, owners), jnp.int32),
            pltpu.VMEM((side, side, q_dev * q_tokens, dim), jnp.bfloat16),
            pltpu.VMEM((2, held, xs, block, dim), jnp.bfloat16),
            pltpu.VMEM((2, side, side, 1, 128), jnp.float32),
            pltpu.VMEM((owners, 1, 128), jnp.float32),
            pltpu.VMEM((owners, 128), jnp.int32),
            pltpu.VMEM((xs, slots, owners), jnp.float32),
            dma((5,)), dma, dma, dma, dma, dma, dma, dma((side,)), dma, dma,
            dma((xs,)), dma((xs,)), dma, dma, dma, dma((xs,)), dma((xs,)),
        ],
        compiler_params=pltpu.CompilerParams(
            collective_id=0, has_side_effects=True, vmem_limit_bytes=60 * 2**20),
        cost_estimate=pl.CostEstimate(
            flops=2 * per_owner * block * owners * q_dev * q_tokens * dim, bytes_accessed=8 * 2**20,
            transcendentals=0),
    )(queries.reshape(q_dev * q_tokens, dim), passages, lengths,
      pair_query.T, pair_passage.T, send_counts.reshape(1, owners))
    return out.T


def solution(mesh):
    placed = (
        P("shard", None, None),
        P("shard", "blk", None),
        P("shard"),
        P("shard", None),
        P("shard", None),
        P("shard"),
    )
    side = math.isqrt(mesh.shape["shard"] // 2)
    return jax.shard_map(
        functools.partial(local, side, mesh.shape["blk"]),
        mesh=mesh, in_specs=placed, out_specs=P("shard", None), check_vma=False
    )
```

```python
import functools
import math

import jax
import jax.numpy as jnp
from jax import lax
from jax.experimental import pallas as pl
from jax.experimental.pallas import tpu as pltpu
from jax.sharding import PartitionSpec as P

NT = (((1,), (1,)), ((), ()))


def kernel(side, xs, q_dev, q_hbm, p_hbm, len_hbm, pq_hbm, pp_hbm, cnt_hbm, o_ref,
           len_ref, len_far, pq_ref, pp_ref, cnt_ref, qs, raw, ps, maxima, rows, table, idx, outs,
           in_sems, len_send, len_recv, near_send, near_recv, line_send, line_recv, sib_send, sib_recv,
           px_send, px_recv, px_local, row_send, row_recv, out_send, out_recv):
    me = lax.axis_index("shard")
    x = lax.axis_index("blk")
    core = me % 2
    zz = (me // 2) % side
    yy = me // (2 * side)
    f = zz + core * (yy - zz)
    g = yy + core * (zz - yy)

    def wrap(value, size):
        return (value + 2 * size) % size

    def at(ff, gg):
        ff, gg = wrap(ff, side), wrap(gg, side)
        return {"shard": core + ff * (2 + core * (2 * side - 2)) + gg * (2 * side - core * (2 * side - 2))}

    def along_x(o):
        return {"blk": wrap(x + o, xs)}

    sibling = {"shard": me + 1 - 2 * core}

    def remote(src, dst, send, recv, to):
        return pltpu.make_async_remote_copy(src_ref=src, dst_ref=dst, send_sem=send, recv_sem=recv,
                                            device_id=to, device_id_type=pl.DeviceIdType.MESH)

    barrier = pltpu.get_barrier_semaphore()
    friends = ([along_x(o) for o in (2, 1, 3)] + [at(f + o, g) for o in (4, 3, 5, 2, 6, 1, 7)]
               + [at(f, g + o) for o in (4, 3, 5, 2, 6, 1, 7)] + [sibling])
    for friend in friends:
        pl.semaphore_signal(barrier, inc=1, device_id=friend, device_id_type=pl.DeviceIdType.MESH)
    sources = [(len_hbm, len_ref), (pq_hbm, pq_ref), (pp_hbm, pp_ref), (cnt_hbm, cnt_ref), (q_hbm, qs.at[zz, yy])]
    small = [pltpu.make_async_copy(src, dst, in_sems.at[i]) for i, (src, dst) in enumerate(sources)]
    for copy in small:
        copy.start()

    pl.semaphore_wait(barrier, len(friends))

    held = ps.shape[1]
    q_rows = q_hbm.shape[0]

    px = [remote(p_hbm.at[pl.ds(wrap(x + o, xs) * held, held)], raw.at[core, x], px_send.at[o], px_recv.at[o],
                 along_x(o)) for o in range(1, xs)]
    for o in (2, 1, 3):
        px[o - 1].start()
    for o in range(1, side):
        remote(q_hbm, qs.at[zz, yy], near_send, near_recv.at[f], at(f + o, g)).start()
    own = p_hbm.at[pl.ds(x * held, held)]
    px_own = pltpu.make_async_copy(own, raw.at[core, x], px_local)
    px_own.start()

    def block(o):
        return raw.at[core, wrap(x - o, xs)]

    share = [remote(own, block(0), sib_send.at[0], sib_recv.at[0], sibling)]
    share += [remote(block(o), block(o), sib_send.at[o], sib_recv.at[o], sibling) for o in range(1, xs)]
    share[0].start()
    lens_out = remote(len_hbm, len_far, len_send, len_recv, sibling)
    lens_out.start()

    for copy in small:
        copy.wait()
    slots = pq_ref.shape[0]
    wanted = pq_ref[...] * (held * xs) + pp_ref[...]
    owners = wanted.shape[1]
    wanted = jnp.concatenate([wanted, jnp.zeros((128 - slots, owners), jnp.int32)], axis=0)
    idx[...] = wanted.T

    n = side * q_rows
    tokens = q_rows // q_dev
    lane = lax.broadcasted_iota(jnp.int32, (q_dev * side, n), 1)
    line = lax.broadcasted_iota(jnp.int32, (q_dev * side, n), 0)
    member = jnp.where((line % side) * q_dev + line // side == lane // tokens, 1.0, 0.0).astype(jnp.bfloat16)

    plen = ps.shape[2] * ps.shape[3]
    dim = ps.shape[4]

    def best_match(gg):
        sims = lax.dot_general(ps[...].reshape(2 * held * plen, dim), qs[gg].reshape(n, dim), NT,
                               preferred_element_type=jnp.float32)
        return jnp.max(sims.reshape(2 * held, plen, n), axis=1)

    def add_up(best, gg):
        high = best.astype(jnp.bfloat16)
        rest = best - high.astype(jnp.float32)
        mid = rest.astype(jnp.bfloat16)
        low = (rest - mid.astype(jnp.float32)).astype(jnp.bfloat16)
        total = (lax.dot_general(member, high, NT, preferred_element_type=jnp.float32)
                 + lax.dot_general(member, mid, NT, preferred_element_type=jnp.float32)
                 + lax.dot_general(member, low, NT, preferred_element_type=jnp.float32))
        blank = jnp.zeros((side, 128 - held), jnp.float32)
        for c in range(2):
            line_w = jnp.zeros((side, 128), jnp.float32)
            for q in range(q_dev):
                part = total[q * side:(q + 1) * side, c * held:(c + 1) * held]
                part = jnp.concatenate([part, blank], axis=1)
                line_w = line_w + pltpu.roll(part, q * held * xs + x * held, 1)
            rows[c, gg] = line_w.reshape(side, 1, 128)

    mine = table.at[pl.ds(2 * (me // 2), 2)]

    def owner_at(y, z):
        return {"shard": (y * side + z) * 2 + core}

    def send_rows(z):
        for o in range(1, side):
            y = wrap(yy + o, side)
            remote(rows.at[:, z, y], mine, row_send, row_recv, owner_at(y, z)).start()

        @pl.when(z != zz)
        def _():
            remote(rows.at[:, z, yy], mine, row_send, row_recv, owner_at(yy, z)).start()

    def near_arrived(ff):
        block = qs.at[zz, yy]
        remote(block, block, near_send, near_recv.at[ff], sibling).wait_recv()

    @pl.when(core == 1)
    def _():
        for o in range(1, side):
            near_arrived(wrap(f + o, side))
        for o in (1, -1, 2, -2):
            remote(qs.at[zz], qs.at[zz], line_send, line_recv.at[zz], at(f, g + o)).start()

    @pl.when(core == 0)
    def _():
        for z in range(0, side, 2):
            for ff in (z, z + 1):
                @pl.when(ff != f)
                def _():
                    near_arrived(ff)
            pair = qs.at[pl.ds(z, 2), yy]
            for o in (4, 3, 5, 2, 6, 1, 7):
                remote(pair, pair, line_send, line_recv.at[z], at(f, g + o)).start()

    for o in (1, 3, 2):
        px[o - 1].wait_recv()
        share[o].start()
    px_own.wait()

    def pad(owner, counts):
        token = lax.broadcasted_iota(jnp.int32, (plen, dim), 0)

        def one(i, _):
            vectors = raw[owner, :, i].reshape(plen, dim).astype(jnp.float32)
            kept = jnp.where(token < counts[x * held + i], vectors, vectors[0:1, :])
            ps[owner, i] = kept.astype(jnp.bfloat16).reshape(ps.shape[2:])
            return 0
        lax.fori_loop(0, held, one, 0, unroll=4)

    pad(core, len_ref)
    lens_out.wait_recv()
    for copy in share:
        copy.wait_recv()
    pad(1 - core, len_far)

    maxima[...] = jnp.zeros_like(maxima)

    def line_arrived(z):
        remote(qs.at[z], qs.at[z], line_send, line_recv.at[z], sibling).wait_recv()

    def step(z, _):
        @pl.when(jnp.logical_and(core == 1, z == 0))
        def _():
            for way in (1, -1):
                far = wrap(zz - 2 * way, side)
                line_arrived(far)
                remote(qs.at[far], qs.at[far], line_send, line_recv.at[far], at(f, g + way)).start()
                part = qs.at[far, pl.ds(0 if way == 1 else side // 2, side // 2)]
                remote(part, part, line_send, line_recv.at[far], at(f, g + 2 * way)).start()

        apart = wrap(z - zz, side)

        @pl.when(jnp.logical_and(core == 1, jnp.logical_and(apart != 0, jnp.logical_and(
            apart != 2, apart != side - 2))))
        def _():
            line_arrived(z)

        @pl.when(jnp.logical_and(core == 0, z % 2 == 0))
        def _():
            pairs = qs.at[pl.ds(0, 2), pl.ds(0, side - 1)]
            remote(pairs, pairs, line_send, line_recv.at[z], sibling).wait_recv()
        before = jnp.maximum(z - 1, 0)
        last = maxima[...]
        maxima[...] = best_match(z)
        add_up(last, before)

        @pl.when(z > 0)
        def _():
            send_rows(before)
        return 0
    lax.fori_loop(0, side, step, 0)
    add_up(maxima[...], side - 1)
    send_rows(side - 1)
    table[pl.ds(2 * (me // 2), 2)] = rows[:, zz, yy]

    rest = table.at[pl.ds(0, owners - 2)]
    remote(rest, rest, row_send, row_recv, sibling).wait_recv()
    picked = jnp.take_along_axis(table[...].reshape(owners, 128), idx[...], axis=1, mode="promise_in_bounds")
    picked = picked.T[:slots, :]
    slot = lax.broadcasted_iota(jnp.int32, (slots, owners), 0)
    outs[0] = jnp.where(slot < cnt_ref[...], picked, 0.0)
    out_copies = [remote(outs.at[0], outs.at[o], out_send.at[o], out_recv.at[o], along_x(o)) for o in range(1, xs)]
    for copy in out_copies:
        copy.start()
    total = outs[0]
    for o, copy in zip(range(1, xs), out_copies):
        copy.wait_recv()
        total = total + outs[o]
    o_ref[...] = total

    for copy in out_copies + px + share + [lens_out]:
        copy.wait_send()
    blocks = qs.at[0, pl.ds(0, side - 1)]
    remote(blocks, blocks, near_send, near_recv.at[0], sibling).wait_send()
    lines = qs.at[pl.ds(0, side - 1)]
    remote(lines, lines, line_send, line_recv.at[0], sibling).wait_send()
    remote(rest, rest, row_send, row_recv, sibling).wait_send()


def local(side, xs, queries, passages, lengths, pair_query, pair_passage, send_counts):
    owners, slots = pair_query.shape
    q_dev, q_tokens, dim = queries.shape
    per_owner, block, _ = passages.shape
    held = per_owner // xs
    dma = pltpu.SemaphoreType.DMA
    out = pl.pallas_call(
        functools.partial(kernel, side, xs, q_dev),
        out_shape=jax.ShapeDtypeStruct((slots, owners), jnp.float32),
        in_specs=[pl.BlockSpec(memory_space=pltpu.HBM)] * 6,
        out_specs=pl.BlockSpec(memory_space=pltpu.VMEM),
        scratch_shapes=[
            pltpu.SMEM((per_owner,), jnp.int32),
            pltpu.SMEM((per_owner,), jnp.int32),
            pltpu.VMEM((slots, owners), jnp.int32),
            pltpu.VMEM((slots, owners), jnp.int32),
            pltpu.VMEM((1, owners), jnp.int32),
            pltpu.VMEM((side, side, q_dev * q_tokens, dim), jnp.bfloat16),
            pltpu.VMEM((2, xs, held, block, dim), jnp.bfloat16),
            pltpu.VMEM((2, held, xs, block, dim), jnp.bfloat16),
            pltpu.VMEM((2 * held, side * q_dev * q_tokens), jnp.float32),
            pltpu.VMEM((2, side, side, 1, 128), jnp.float32),
            pltpu.VMEM((owners, 1, 128), jnp.float32),
            pltpu.VMEM((owners, 128), jnp.int32),
            pltpu.VMEM((xs, slots, owners), jnp.float32),
            dma((5,)), dma, dma, dma, dma((side,)), dma, dma((side,)), dma((xs,)), dma((xs,)),
            dma((xs,)), dma((xs,)), dma, dma, dma, dma((xs,)), dma((xs,)),
        ],
        compiler_params=pltpu.CompilerParams(
            collective_id=0, has_side_effects=True, vmem_limit_bytes=60 * 2**20),
        cost_estimate=pl.CostEstimate(
            flops=2 * per_owner * block * owners * q_dev * q_tokens * dim, bytes_accessed=8 * 2**20,
            transcendentals=0),
    )(queries.reshape(q_dev * q_tokens, dim), passages, lengths,
      pair_query.T, pair_passage.T, send_counts.reshape(1, owners))
    return out.T


def solution(mesh):
    placed = (
        P("shard", None, None),
        P("shard", "blk", None),
        P("shard"),
        P("shard", None),
        P("shard", None),
        P("shard"),
    )
    side = math.isqrt(mesh.shape["shard"] // 2)
    return jax.shard_map(
        functools.partial(local, side, mesh.shape["blk"]),
        mesh=mesh, in_specs=placed, out_specs=P("shard", None), check_vma=False
    )
```

```python
import functools
import math

import jax
import jax.numpy as jnp
from jax import lax
from jax.experimental import pallas as pl
from jax.experimental.pallas import tpu as pltpu
from jax.sharding import PartitionSpec as P

NT = (((1,), (1,)), ((), ()))


def kernel(side, xs, q_dev, q_hbm, p_hbm, len_hbm, pq_hbm, pp_hbm, cnt_hbm, o_ref,
           len_ref, len_far, pq_ref, pp_ref, cnt_ref, qs, raw, ps, maxima, rows, table, idx, outs,
           in_sems, len_send, len_recv, near_send, near_recv, line_send, line_recv, hand_send, sib_send, sib_recv,
           px_send, px_recv, px_local, row_send, row_recv, out_send, out_recv):
    me = lax.axis_index("shard")
    x = lax.axis_index("blk")
    core = me % 2
    zz = (me // 2) % side
    yy = me // (2 * side)
    f = zz + core * (yy - zz)
    g = yy + core * (zz - yy)

    def wrap(value, size):
        return (value + 2 * size) % size

    def at(ff, gg):
        ff, gg = wrap(ff, side), wrap(gg, side)
        return {"shard": core + ff * (2 + core * (2 * side - 2)) + gg * (2 * side - core * (2 * side - 2))}

    def along_x(o):
        return {"blk": wrap(x + o, xs)}

    sibling = {"shard": me + 1 - 2 * core}

    def remote(src, dst, send, recv, to):
        return pltpu.make_async_remote_copy(src_ref=src, dst_ref=dst, send_sem=send, recv_sem=recv,
                                            device_id=to, device_id_type=pl.DeviceIdType.MESH)

    barrier = pltpu.get_barrier_semaphore()
    friends = ([along_x(o) for o in (2, 1, 3)] + [at(f + o, g) for o in (4, 3, 5, 2, 6, 1, 7)]
               + [at(f, g + o) for o in (4, 3, 5, 2, 6, 1, 7)] + [sibling])
    for friend in friends:
        pl.semaphore_signal(barrier, inc=1, device_id=friend, device_id_type=pl.DeviceIdType.MESH)
    sources = [(len_hbm, len_ref), (pq_hbm, pq_ref), (pp_hbm, pp_ref), (cnt_hbm, cnt_ref), (q_hbm, qs.at[zz, yy])]
    small = [pltpu.make_async_copy(src, dst, in_sems.at[i]) for i, (src, dst) in enumerate(sources)]
    for copy in small:
        copy.start()

    pl.semaphore_wait(barrier, len(friends))

    held = ps.shape[1]
    q_rows = q_hbm.shape[0]

    px = [remote(p_hbm.at[pl.ds(wrap(x + o, xs) * held, held)], raw.at[core, x], px_send.at[o], px_recv.at[o],
                 along_x(o)) for o in range(1, xs)]
    for o in (2, 1, 3):
        px[o - 1].start()
    for o in range(1, side):
        remote(q_hbm, qs.at[zz, yy], near_send, near_recv.at[f], at(f + o, g)).start()
    own = p_hbm.at[pl.ds(x * held, held)]
    px_own = pltpu.make_async_copy(own, raw.at[core, x], px_local)
    px_own.start()

    def block(o):
        return raw.at[core, wrap(x - o, xs)]

    share = [remote(own, block(0), sib_send.at[0], sib_recv.at[0], sibling)]
    share += [remote(block(o), block(o), sib_send.at[o], sib_recv.at[o], sibling) for o in range(1, xs)]
    share[0].start()
    lens_out = remote(len_hbm, len_far, len_send, len_recv, sibling)
    lens_out.start()

    for copy in small:
        copy.wait()
    slots = pq_ref.shape[0]
    wanted = pq_ref[...] * (held * xs) + pp_ref[...]
    owners = wanted.shape[1]
    wanted = jnp.concatenate([wanted, jnp.zeros((128 - slots, owners), jnp.int32)], axis=0)
    idx[...] = wanted.T

    n = side * q_rows
    tokens = q_rows // q_dev
    lane = lax.broadcasted_iota(jnp.int32, (q_dev * side, n), 1)
    line = lax.broadcasted_iota(jnp.int32, (q_dev * side, n), 0)
    member = jnp.where((line % side) * q_dev + line // side == lane // tokens, 1.0, 0.0).astype(jnp.bfloat16)

    plen = ps.shape[2] * ps.shape[3]
    dim = ps.shape[4]

    def best_match(gg, c=None):
        tokens_of = ps[...] if c is None else ps[c]
        count = 2 * held if c is None else held
        sims = lax.dot_general(tokens_of.reshape(count * plen, dim), qs[gg].reshape(n, dim), NT,
                               preferred_element_type=jnp.float32)
        return jnp.max(sims.reshape(count, plen, n), axis=1)

    def add_up(best, gg):
        high = best.astype(jnp.bfloat16)
        rest = best - high.astype(jnp.float32)
        mid = rest.astype(jnp.bfloat16)
        low = (rest - mid.astype(jnp.float32)).astype(jnp.bfloat16)
        total = (lax.dot_general(member, high, NT, preferred_element_type=jnp.float32)
                 + lax.dot_general(member, mid, NT, preferred_element_type=jnp.float32)
                 + lax.dot_general(member, low, NT, preferred_element_type=jnp.float32))
        blank = jnp.zeros((side, 128 - held), jnp.float32)
        for c in range(2):
            line_w = jnp.zeros((side, 128), jnp.float32)
            for q in range(q_dev):
                part = total[q * side:(q + 1) * side, c * held:(c + 1) * held]
                part = jnp.concatenate([part, blank], axis=1)
                line_w = line_w + pltpu.roll(part, q * held * xs + x * held, 1)
            rows[c, gg] = line_w.reshape(side, 1, 128)

    mine = table.at[pl.ds(2 * (me // 2), 2)]

    def owner_at(y, z):
        return {"shard": (y * side + z) * 2 + core}

    def send_rows(z):
        for o in (4, 3, 5, 2, 6, 1, 7):
            y = wrap(yy + o, side)
            remote(rows.at[:, z, y], mine, row_send, row_recv, owner_at(y, z)).start()

        @pl.when(z != zz)
        def _():
            remote(rows.at[:, z, yy], mine, row_send, row_recv, owner_at(yy, z)).start()

    def near_arrived(ff):
        block = qs.at[zz, yy]
        remote(block, block, near_send, near_recv.at[ff], sibling).wait_recv()

    @pl.when(core == 1)
    def _():
        for o in range(1, side):
            near_arrived(wrap(f + o, side))
        for o in (2, -2, 1, -1):
            remote(qs.at[zz], qs.at[zz], line_send, line_recv.at[zz], at(f, g + o)).start()

    @pl.when(core == 0)
    def _():
        for z in range(0, side - 2, 2):
            for ff in (z, z + 1):
                @pl.when(ff != f)
                def _():
                    near_arrived(ff)
            pair = qs.at[pl.ds(z, 2), yy]
            for o in (4, 3, 5, 2, 6, 1, 7):
                remote(pair, pair, line_send, line_recv.at[z], at(f, g + o)).start()

    def last_pair():
        for ff in (side - 2, side - 1):
            @pl.when(ff != f)
            def _():
                near_arrived(ff)
        pair = qs.at[pl.ds(side - 2, 2), yy]
        for o in (4, 3, 5, 2, 6, 1, 7):
            remote(pair, pair, line_send, line_recv.at[side - 2], at(f, g + o)).start()

    for o in (1, 3, 2):
        px[o - 1].wait_recv()
        share[o].start()
    px_own.wait()

    def pad(owner, counts):
        token = lax.broadcasted_iota(jnp.int32, (plen, dim), 0)

        def one(i, _):
            vectors = raw[owner, :, i].reshape(plen, dim).astype(jnp.float32)
            kept = jnp.where(token < counts[x * held + i], vectors, vectors[0:1, :])
            ps[owner, i] = kept.astype(jnp.bfloat16).reshape(ps.shape[2:])
            return 0
        lax.fori_loop(0, held, one, 0, unroll=4)

    def line_arrived(z):
        remote(qs.at[z], qs.at[z], line_send, line_recv.at[z], sibling).wait_recv()

    def handed_on(way):
        far = wrap(zz - 2 * way, side)
        part = qs.at[far, pl.ds(0 if way == 1 else side // 2, side // 2)]
        return far, [remote(qs.at[far], qs.at[far], hand_send.at[(way + 1) // 2], line_recv.at[far], at(f, g + way)),
                     remote(part, part, hand_send.at[(way + 1) // 2], line_recv.at[far], at(f, g + 2 * way))]

    hands = [handed_on(1), handed_on(-1)]

    def apart(z):
        return wrap(z - zz, side)

    def key(z):
        distant = jnp.logical_and(apart(z) > 2, apart(z) < side - 2)
        return 4 * z + jnp.where(jnp.logical_and(core == 1, distant), (14, 11, 10, 9)[z] if z < 4 else 14, 0)

    keys = [key(z) for z in range(side)]
    ranks = [sum(jnp.where(other < mine_, 1, 0) for other in keys) for mine_ in keys]
    order = [sum(jnp.where(rank == i, z, 0) for z, rank in enumerate(ranks)) for i in range(side)]

    def fetch(i):
        z = sum(jnp.where(i == at_, place, 0) for at_, place in enumerate(order))

        got = jnp.logical_or(apart(z) == 2, apart(z) == side - 2)

        @pl.when(jnp.logical_and(core == 1, jnp.logical_and(z != zz, jnp.logical_not(got))))
        def _():
            line_arrived(z)

        @pl.when(jnp.logical_and(core == 0, z % 2 == 0))
        def _():
            pairs = qs.at[pl.ds(0, 2), pl.ds(0, side - 1)]
            remote(pairs, pairs, line_send, line_recv.at[z], sibling).wait_recv()
        return z

    pad(core, len_ref)

    def hand_on(early):
        for far, copies in hands:
            @pl.when(jnp.logical_and(core == 1, (far < side // 2) == early))
            def _():
                line_arrived(far)
                for copy in copies:
                    copy.start()

    hand_on(True)

    first = fetch(0)
    maxima[pl.ds(pl.multiple_of(core * held, 8), held)] = best_match(first, core)
    lens_out.wait_recv()
    for copy in share:
        copy.wait_recv()
    pad(1 - core, len_far)
    maxima[pl.ds(pl.multiple_of((1 - core) * held, 8), held)] = best_match(first, 1 - core)
    add_up(maxima[...], first)
    send_rows(first)
    pl.when(core == 0)(last_pair)
    hand_on(False)

    def step(i, _):
        z = fetch(i)
        add_up(best_match(z), z)
        send_rows(z)
        return 0
    lax.fori_loop(1, side, step, 0)
    table[pl.ds(2 * (me // 2), 2)] = rows[:, zz, yy]

    rest = table.at[pl.ds(0, owners - 2)]
    remote(rest, rest, row_send, row_recv, sibling).wait_recv()
    picked = jnp.take_along_axis(table[...].reshape(owners, 128), idx[...], axis=1, mode="promise_in_bounds")
    picked = picked.T[:slots, :]
    slot = lax.broadcasted_iota(jnp.int32, (slots, owners), 0)
    outs[0] = jnp.where(slot < cnt_ref[...], picked, 0.0)
    out_copies = [remote(outs.at[0], outs.at[o], out_send.at[o], out_recv.at[o], along_x(o)) for o in range(1, xs)]
    for o in (2, 1, 3):
        out_copies[o - 1].start()
    total = outs[0]
    for o, copy in zip(range(1, xs), out_copies):
        copy.wait_recv()
        total = total + outs[o]
    o_ref[...] = total

    for copy in out_copies + px + share + [lens_out]:
        copy.wait_send()
    blocks = qs.at[0, pl.ds(0, side - 1)]
    remote(blocks, blocks, near_send, near_recv.at[0], sibling).wait_send()
    for count, which in ((side - 1, core == 0), (4, core == 1)):
        @pl.when(which)
        def _():
            lines = qs.at[pl.ds(0, count)]
            remote(lines, lines, line_send, line_recv.at[0], sibling).wait_send()
    for way in range(2):
        @pl.when(core == 1)
        def _():
            amount = qs.at[pl.ds(0, 3), pl.ds(0, side // 2)]
            remote(amount, amount, hand_send.at[1 - way], line_recv.at[0], sibling).wait_send()
    remote(rest, rest, row_send, row_recv, sibling).wait_send()


def local(side, xs, queries, passages, lengths, pair_query, pair_passage, send_counts):
    owners, slots = pair_query.shape
    q_dev, q_tokens, dim = queries.shape
    per_owner, block, _ = passages.shape
    held = per_owner // xs
    dma = pltpu.SemaphoreType.DMA
    out = pl.pallas_call(
        functools.partial(kernel, side, xs, q_dev),
        out_shape=jax.ShapeDtypeStruct((slots, owners), jnp.float32),
        in_specs=[pl.BlockSpec(memory_space=pltpu.HBM)] * 6,
        out_specs=pl.BlockSpec(memory_space=pltpu.VMEM),
        scratch_shapes=[
            pltpu.SMEM((per_owner,), jnp.int32),
            pltpu.SMEM((per_owner,), jnp.int32),
            pltpu.VMEM((slots, owners), jnp.int32),
            pltpu.VMEM((slots, owners), jnp.int32),
            pltpu.VMEM((1, owners), jnp.int32),
            pltpu.VMEM((side, side, q_dev * q_tokens, dim), jnp.bfloat16),
            pltpu.VMEM((2, xs, held, block, dim), jnp.bfloat16),
            pltpu.VMEM((2, held, xs, block, dim), jnp.bfloat16),
            pltpu.VMEM((2 * held, side * q_dev * q_tokens), jnp.float32),
            pltpu.VMEM((2, side, side, 1, 128), jnp.float32),
            pltpu.VMEM((owners, 1, 128), jnp.float32),
            pltpu.VMEM((owners, 128), jnp.int32),
            pltpu.VMEM((xs, slots, owners), jnp.float32),
            dma((5,)), dma, dma, dma, dma((side,)), dma, dma((side,)), dma((2,)), dma((xs,)), dma((xs,)),
            dma((xs,)), dma((xs,)), dma, dma, dma, dma((xs,)), dma((xs,)),
        ],
        compiler_params=pltpu.CompilerParams(
            collective_id=0, has_side_effects=True, vmem_limit_bytes=60 * 2**20),
        cost_estimate=pl.CostEstimate(
            flops=2 * per_owner * block * owners * q_dev * q_tokens * dim, bytes_accessed=8 * 2**20,
            transcendentals=0),
    )(queries.reshape(q_dev * q_tokens, dim), passages, lengths,
      pair_query.T, pair_passage.T, send_counts.reshape(1, owners))
    return out.T


def solution(mesh):
    placed = (
        P("shard", None, None),
        P("shard", "blk", None),
        P("shard"),
        P("shard", None),
        P("shard", None),
        P("shard"),
    )
    side = math.isqrt(mesh.shape["shard"] // 2)
    return jax.shard_map(
        functools.partial(local, side, mesh.shape["blk"]),
        mesh=mesh, in_specs=placed, out_specs=P("shard", None), check_vma=False
    )
```
